32 devices in a mesh: groups: 2 (over y), workers: 4 (over z), team: 2 (over x), sub: 2 (over core).
Axes of the slice: x: 2, y: 2, z: 4, core: 2. Of those that a mesh axis runs over, the one named last changes fastest.
Arguments:
- embeddings: bfloat16 [8192, 1024], P(('groups', 'workers', 'team', 'sub')), parts along dimension 0, may hold values from -6 to 6
- owner_ids: int32 [8192, 1], P(('groups', 'workers', 'team', 'sub')), parts along dimension 0, may hold values from 0 to 3; in each aligned block of 256 rows (0 to 255, 256 to 511, ...) at most 160 rows name the same one
- clusters: int32 [8192], P(('groups', 'workers', 'team', 'sub')), parts along dimension 0, may hold values from 0 to 15
- priority: int32 [8192], P(('groups', 'workers', 'team', 'sub')), parts along dimension 0, may hold values from 0 to 4095, each once
Outputs:
- max_similarity: float32 [8192], P(('groups', 'workers', 'team', 'sub')), parts along dimension 0
The draws below stay inside these ranges and needn't reach their ends.
There are 2 independent parts, one for each index of `groups`. The reference program is written for one: setup_inputs(seed, part) draws one part's arguments, and reference() takes and returns one part's arrays. A program takes and returns all parts, laid end to end along the dimension named above; each array names one. Nothing has to cross between parts.
Inputs may be any that keep to these rules, and one draw needn't show every extreme that they name: `owner_ids`: in the rows of one device no worker is named by more than 160 rows, a bound that some block reaches of them. `priority`: within one part every value appears exactly once.
All inputs are finite; a program needn't handle non-finite values.
Results may differ from the reference program's by a relative error of at most 0.0009.
Values may be sent and summed in bfloat16 or wider, within the bound.
No kernel may reach another device: no remote copies, remote signals or barrier semaphores. Data moves between devices by JAX's collectives and lax.ppermute only.
A program may use at most 64 MiB of HBM per device.

```python
import math
import jax
import jax.numpy as jnp
import numpy as np
from jax import lax

E = 1024
ROWS_DEV = 256
KC = 16
CAP = 160
ROWS = 4096
N_WORKERS = 4
N_TEAM = 2
N_SUB = 2


def with_ends(values, key, low, high):
    longest = values.shape.index(max(values.shape))
    spots = []
    for shift in (0, 1):
        where = [jax.random.randint(jax.random.fold_in(key, axis), (), 0, length) for axis, length in enumerate(values.shape)]
        where[longest] = (where[longest] + shift) % values.shape[longest]
        spots.append(tuple(where))
    return values.at[spots[0]].set(low).at[spots[1]].set(high)


def levels(own_key, extent, shards, low, high):
    factor_of = 1.0
    for axis_at, shards_of in shards:
        draws = jax.random.uniform(jax.random.fold_in(jax.random.fold_in(own_key, 6), axis_at), (shards_of,), jnp.float32, low / len(shards), high / len(shards))
        factor_of = factor_of * jnp.repeat(jnp.exp(draws), extent[axis_at] // shards_of).reshape((-1,) + (1,) * (len(extent) - 1 - axis_at))
    return factor_of


def rank_bounds(count, lean):
    weights = [(1 << 20) // math.isqrt(grade ** lean) + 1 for grade in range(1, count + 1)]
    spread = 1 + sum(weights) // (1 << 30)
    return np.cumsum(np.array([max(1, weight // spread) for weight in weights]))


def ranked_ids(stream_key, shape, amount, skew):
    table = rank_bounds(amount, skew)
    lot = jax.random.randint(jax.random.fold_in(stream_key, 1), shape, 0, int(table[amount - 1]))
    rank = jnp.searchsorted(jnp.asarray(table, jnp.int32), lot, side="right")
    return jax.random.permutation(jax.random.fold_in(stream_key, 2), amount)[rank].astype(jnp.int32)


def assign_block(stream_key, own, number, rows, number_of, top, bound, lean):
    sequence = jax.random.permutation(stream_key, number_of)
    crowded, common = load_shares(number_of, rows * top, bound, lean, True), load_shares(number_of, rows * top, bound, lean, False)
    places = jnp.arange(number_of)

    def named(lengths, turn):
        used = int((lengths > 0).sum())
        fixed = max(1, used // 4)
        moved = fixed + (places - fixed + turn * (used - fixed)) % max(1, number_of - fixed)
        return jnp.zeros((number_of,), jnp.int32).at[sequence[jnp.where(places < fixed, places, moved)]].set(jnp.asarray(lengths, jnp.int32))

    lengths = jnp.where(number % 4 == 0, named(crowded, number // 4), named(common, number - number // 4 - 1))
    mixed = jax.random.permutation(jax.random.fold_in(own, 3), number_of)
    donor, sink = mixed[0:number_of // 2 * 2:2], mixed[1:number_of // 2 * 2:2]
    margin = jnp.minimum(lengths[donor] - 1, bound - lengths[sink]) // 2
    margin = jnp.where((donor == sequence[0]) | (sink == sequence[0]) | (lengths[sink] == 0), 0, jnp.maximum(margin, 0))
    moved = jax.random.randint(jax.random.fold_in(own, 4), (number_of // 2,), 0, 1 << 20) % (margin + 1)
    lengths = lengths.at[donor].add(-moved).at[sink].add(moved)
    members = jnp.searchsorted(jnp.cumsum(lengths), jnp.arange(rows * top), side="right").astype(jnp.int32)
    listing = members.reshape(top, rows).T
    listing = listing[jax.random.permutation(jax.random.fold_in(own, 1), rows)]
    turn = jax.random.randint(jax.random.fold_in(own, 2), (rows, 1), 0, top)
    return jnp.take_along_axis(listing, (jnp.arange(top)[None, :] + turn) % top, axis=1)


def load_shares(number_of, total, reach, lean, full):
    portions = [(1 << 20) // math.isqrt(rank ** lean) + 1 for rank in range(1, number_of + 1)]
    largest = reach if full else min(reach, max(-(-total // number_of), total * portions[0] // sum(portions)))
    least = 1 if total - largest >= number_of - 1 else 0
    given, spare = [largest] + [least] * (number_of - 1), total - largest - least * (number_of - 1)
    while spare > 0:
        candidates = [i for i in range(1, number_of) if given[i] < largest] or [i for i in range(1, number_of) if given[i] < reach]
        whole, left = sum([portions[i] for i in candidates]), spare
        for i in candidates:
            extra = min(reach - given[i], max(1, left * portions[i] // whole), spare)
            given[i] = given[i] + extra
            spare = spare - extra
    return np.array(given)


def normal_values(own_key, dims, width, reach, pieces=(), held_as=jnp.bfloat16):
    level = levels(own_key, dims, pieces, -0.22, 0.18) if pieces else 1.0
    result = jax.random.normal(own_key, dims, jnp.float32) * width * level
    return jnp.minimum(jnp.maximum(result, -reach), reach).astype(held_as)


def setup_inputs(seed: int = 0, part: int = 0) -> dict:
    keys = jax.random.split(jax.random.key(seed), 5)
    part_keys = jax.random.split(jax.random.fold_in(keys[4], part), 5)
    embeddings = normal_values(part_keys[0], (ROWS, E), 1.0, 6.0, ((0, 16),))
    owner_ids_keys = jax.random.split(jax.random.fold_in(part_keys[1], 1), ROWS // ROWS_DEV)
    owner_ids_turns = jax.random.permutation(jax.random.fold_in(part_keys[1], 3), ROWS // ROWS_DEV)
    owner_ids = jax.vmap(lambda own, number: assign_block(jax.random.fold_in(part_keys[1], 2), own, number, ROWS_DEV, N_WORKERS, 1, CAP, 2))(owner_ids_keys, owner_ids_turns).reshape((ROWS, 1))
    clusters = with_ends(ranked_ids(part_keys[2], (ROWS,), KC, 2), jax.random.fold_in(part_keys[2], 3), 0, KC - 1).astype(jnp.int32)
    priority = jax.random.permutation(part_keys[3], ROWS).astype(jnp.int32)
    return {"embeddings": embeddings, "owner_ids": owner_ids, "clusters": clusters, "priority": priority}


def reference(embeddings, owner_ids, clusters, priority):
    values = embeddings.astype(jnp.float32)
    normed = (values * lax.rsqrt(lax.optimization_barrier(jnp.sum(values * values, axis=1, keepdims=True)) + 1e-06)).astype(jnp.bfloat16)
    owner = owner_ids[:, 0].astype(jnp.int32)
    order = jnp.argsort(owner, stable=True).astype(jnp.int32)
    counts = lax.optimization_barrier(jnp.sum((owner[:, None] == jnp.arange(N_WORKERS, dtype=jnp.int32)[None, :]).astype(jnp.int32), axis=0)).astype(jnp.int32)
    starts = (jnp.cumsum(counts) - counts).astype(jnp.int32)
    window = N_WORKERS * N_TEAM * N_SUB * CAP
    block = math.gcd(window, 512)
    sorted_rows = jnp.concatenate([normed[order], jnp.zeros((window, E), jnp.bfloat16)], axis=0)
    sorted_clus = jnp.concatenate([clusters[order], -jnp.ones((window,), jnp.int32)], axis=0)
    sorted_prio = jnp.concatenate([priority[order], jnp.zeros((window,), jnp.int32)], axis=0)

    def per_owner(worker):
        start = starts[worker]
        count = counts[worker]
        rows = lax.dynamic_slice_in_dim(sorted_rows, start, window, 0)
        clus = lax.dynamic_slice_in_dim(sorted_clus, start, window, 0)
        prio = lax.dynamic_slice_in_dim(sorted_prio, start, window, 0)
        valid = jnp.arange(window, dtype=jnp.int32) < count

        def live(index):
            first = (index * block).astype(jnp.int32)
            query = lax.dynamic_slice_in_dim(rows, first, block, 0)
            qclus = lax.dynamic_slice_in_dim(clus, first, block, 0)
            qprio = lax.dynamic_slice_in_dim(prio, first, block, 0)
            scores = lax.dot_general(query, rows, (((1,), (1,)), ((), ())), preferred_element_type=jnp.float32)
            mask = (qclus[:, None] == clus[None, :]) & (prio[None, :] < qprio[:, None]) & valid[None, :]
            return lax.optimization_barrier(jnp.max(jnp.where(mask, scores, jnp.float32(-1.0)), axis=1))

        def per_block(index):
            return lax.cond(index * block < count, live, lambda i: -jnp.ones((block,), jnp.float32), index)
        return lax.map(per_block, jnp.arange(window // block, dtype=jnp.int32)).reshape(window)
    results = lax.map(per_owner, jnp.arange(N_WORKERS, dtype=jnp.int32))
    places = jnp.arange(ROWS, dtype=jnp.int32)
    sorted_owner = owner[order]
    flat = (sorted_owner * window + places - starts[sorted_owner]).astype(jnp.int32)
    found = results.reshape(-1)[flat]
    return jnp.zeros((ROWS,), jnp.float32).at[order].set(found)
```

```python
import functools

import jax
import jax.numpy as jnp
from jax import lax
from jax.experimental import pallas as pl
from jax.experimental.pallas import tpu as pltpu
from jax.sharding import PartitionSpec as P

KC = 16
VMEM = pl.BlockSpec(memory_space=pltpu.VMEM)


def normalise(raw):
    values = raw.astype(jnp.float32)
    total = jnp.sum(values * values, axis=1, keepdims=True)
    return (values * lax.rsqrt(total + 1e-06)).astype(jnp.bfloat16)


def code_of(owner, cluster, high, low):
    return ((owner * KC + cluster) * 256 + high) * 256 + low


def payload_code(ref, rows):
    meta = ref[rows : rows + 16, :].astype(jnp.float32)[0:1, :].astype(jnp.int32)
    return code_of(*[meta[:, i * rows : (i + 1) * rows] for i in range(4)])


def as_column(row):
    return jnp.broadcast_to(row, (128, row.shape[1])).T


def fold_rows(best):
    return jnp.max(best.T, axis=0, keepdims=True)


def prepare_kernel(rows, emb, owner, cluster, priority, payload, meta):
    payload[0:rows, :] = normalise(emb[...])
    own = owner[...] + 1
    high = priority[...] // 256
    low = priority[...] % 256
    line = jnp.concatenate([own, cluster[...], high, low], axis=1).astype(jnp.float32)
    width = payload.shape[1]
    first = lax.broadcasted_iota(jnp.int32, (16, width), 0) == 0
    payload[rows : rows + 16, :] = jnp.where(
        first, jnp.broadcast_to(line, (16, width)), 0.0
    ).astype(jnp.bfloat16)
    meta[...] = jnp.concatenate(
        [own, cluster[...], priority[...], jnp.zeros((5, rows), jnp.int32)], axis=0
    )


def scores_of(left, right):
    return lax.dot_general(
        left, right, (((1,), (1,)), ((), ())), preferred_element_type=jnp.float32
    )


def own_kernel(rows, n_plane, *refs):
    plane, best = refs[:n_plane], refs[n_plane]
    mine = plane[0][0:rows, :]
    column = as_column(payload_code(plane[0], rows))
    found = jnp.full((rows, 128), -1.0, jnp.float32)
    for block in plane:
        scores = scores_of(mine, block[0:rows, :])
        code = payload_code(block, rows)
        for at in range(0, rows, 128):
            other = code[:, at : at + 128]
            earlier = ((column ^ other) < 65536) & (column > other)
            found = jnp.maximum(found, jnp.where(earlier, scores[:, at : at + 128], -1.0))
    best[...] = fold_rows(found)


def meet_kernel(rows, n_plane, raw, *refs):
    plane = refs[:n_plane]
    if raw:
        came, came_meta, back, kept = refs[n_plane:]
        queries = normalise(came[...])
        owner, cluster, priority = [came_meta[i : i + 1, :] for i in range(3)]
        code = code_of(owner, cluster, priority // 256, priority % 256)
    else:
        came, back, kept = refs[n_plane:]
        queries = came[0:rows, :]
        code = payload_code(came, rows)
    column = as_column(code)
    found = jnp.full((rows, 128), -1.0, jnp.float32)
    for index, block in enumerate(plane):
        scores = scores_of(queries, block[0:rows, :])
        code = payload_code(block, rows)
        for at in range(0, rows, 128):
            other = code[:, at : at + 128]
            shared = jnp.where((column ^ other) < 65536, scores[:, at : at + 128], -1.0)
            later = column > other
            found = jnp.maximum(found, jnp.where(later, shared, -1.0))
            kept[index : index + 1, at : at + 128] = jnp.max(
                jnp.where(later, -1.0, shared), axis=0, keepdims=True
            )
    back[...] = fold_rows(found)


def params():
    return pltpu.CompilerParams(vmem_limit_bytes=40 * 1024 * 1024)


def rounds_of(n):
    half = n // 2
    line = [p // 2 + (p % 2) * half for p in range(2 * half)] + list(range(2 * half, n))
    turns = []
    for step in range(1, (n - 1) // 2 + 1):
        turns.append([(line[p], line[(p + step) % n]) for p in range(n)])
    if n % 2 == 0:
        pairs = [(line[p], line[p + half]) for p in range(half)]
        turns.append([(a, b) if i % 2 == 0 else (b, a) for i, (a, b) in enumerate(pairs)])
    return turns


def shift(n, step):
    return [(i, (i + step) % n) for i in range(n)]


def on_device(embeddings, owner_ids, clusters, priority):
    rows, width = embeddings.shape
    n_work, n_team, n_sub = [lax.axis_size(a) for a in ("workers", "team", "sub")]
    n_plane = n_team * n_sub
    turns = rounds_of(n_work)
    first = lax.ppermute(embeddings, "workers", turns[0]) if turns else None

    payload, meta = pl.pallas_call(
        functools.partial(prepare_kernel, rows),
        out_shape=(
            jax.ShapeDtypeStruct((rows + 16, width), jnp.bfloat16),
            jax.ShapeDtypeStruct((8, rows), jnp.int32),
        ),
        in_specs=[VMEM] * 4,
        out_specs=(VMEM, VMEM),
        compiler_params=params(),
        name="prepare",
    )(
        embeddings,
        owner_ids.reshape(1, rows),
        clusters.reshape(1, rows),
        priority.reshape(1, rows),
    )
    came_meta = lax.ppermute(meta, "workers", turns[0]) if turns else None

    by_team = [payload] + [
        lax.ppermute(payload, "team", shift(n_team, step)) for step in range(1, n_team)
    ]
    plane = []
    for block in by_team:
        plane.append(block)
        for step in range(1, n_sub):
            plane.append(lax.ppermute(block, "sub", shift(n_sub, step)))

    best = pl.pallas_call(
        functools.partial(own_kernel, rows, n_plane),
        out_shape=jax.ShapeDtypeStruct((1, rows), jnp.float32),
        in_specs=[VMEM] * n_plane,
        out_specs=VMEM,
        compiler_params=params(),
        name="own",
    )(*plane)

    kept = jnp.full((n_plane, rows), -1.0, jnp.float32)
    for index in list(range(1, len(turns))) + list(range(min(1, len(turns)))):
        turn = turns[index]
        raw = index == 0
        came = (first, came_meta) if raw else (lax.ppermute(payload, "workers", turn),)
        back, part = pl.pallas_call(
            functools.partial(meet_kernel, rows, n_plane, raw),
            out_shape=(
                jax.ShapeDtypeStruct((1, rows), jnp.float32),
                jax.ShapeDtypeStruct((n_plane, rows), jnp.float32),
            ),
            in_specs=[VMEM] * (n_plane + len(came)),
            out_specs=(VMEM, VMEM),
            compiler_params=params(),
            name="meet",
        )(*plane, *came)
        kept = jnp.maximum(kept, part)
        got = lax.ppermute(back, "workers", [(b, a) for a, b in turn])
        if len(turn) < n_work:
            here = lax.axis_index("workers")
            sent = functools.reduce(jnp.logical_or, [here == a for a, _ in turn])
            got = jnp.where(sent, got, -1.0)
        best = jnp.maximum(best, got)

    kept = kept.reshape(n_team, n_sub, rows)
    ends = kept[:, 0]
    for step in range(1, n_sub):
        ends = jnp.maximum(ends, lax.ppermute(kept[:, step], "sub", shift(n_sub, -step)))
    total = ends[0:1]
    for step in range(1, n_team):
        total = jnp.maximum(
            total, lax.ppermute(ends[step : step + 1], "team", shift(n_team, -step))
        )
    return jnp.maximum(best, total).reshape(rows)


def solution(mesh):
    placed = (
        P(("groups", "workers", "team", "sub"), None),
        P(("groups", "workers", "team", "sub"), None),
        P(("groups", "workers", "team", "sub")),
        P(("groups", "workers", "team", "sub")),
    )
    return jax.shard_map(
        on_device,
        mesh=mesh,
        in_specs=placed,
        out_specs=P(("groups", "workers", "team", "sub")),
        check_vma=False,
    )
```

```python
import functools

import jax
import jax.numpy as jnp
from jax import lax
from jax.experimental import pallas as pl
from jax.experimental.pallas import tpu as pltpu
from jax.sharding import PartitionSpec as P

KC = 16
EXTRA = 16
VMEM = pl.BlockSpec(memory_space=pltpu.VMEM)


def normalise(raw):
    values = raw.astype(jnp.float32)
    total = jnp.sum(values * values, axis=1, keepdims=True)
    return (values * lax.rsqrt(total + 1e-06)).astype(jnp.bfloat16)


def code_of(owner, cluster, high, low):
    return ((owner * KC + cluster) * 256 + high) * 256 + low


def code_in(ids):
    place = ids[2:3, :]
    return code_of(ids[0:1, :], ids[1:2, :], place // 256, place % 256)


def code_at(block, rows):
    last = block[rows : rows + EXTRA, :].astype(jnp.float32)[0:1, :].astype(jnp.int32)
    return code_of(*[last[:, i * rows : (i + 1) * rows] for i in range(4)])


def as_column(row):
    return jnp.broadcast_to(row, (128, row.shape[1])).T


def fold_rows(best):
    return jnp.max(best.T, axis=0, keepdims=True)


def scores_of(left, right):
    return lax.dot_general(
        left, right, (((1,), (1,)), ((), ())), preferred_element_type=jnp.float32
    )


def pack_kernel(rows, raw, ids, block):
    width = block.shape[1]
    place = ids[2:3, :]
    line = [ids[0:1, :], ids[1:2, :], place // 256, place % 256]
    line += [jnp.zeros((1, width - 4 * rows), jnp.int32)] if width > 4 * rows else []
    line = jnp.concatenate(line, axis=1).astype(jnp.float32)
    first = lax.broadcasted_iota(jnp.int32, (EXTRA, width), 0) == 0
    last = jnp.where(first, jnp.broadcast_to(line, (EXTRA, width)), 0.0)
    block[0:rows, :] = normalise(raw[...])
    block[rows : rows + EXTRA, :] = last.astype(jnp.bfloat16)


def own_kernel(rows, *refs):
    blocks, (plane, codes, kept) = refs[:-3], refs[-3:]
    mine = blocks[0][0:rows, :]
    column = as_column(code_at(blocks[0], rows))
    found = jnp.full((rows, 128), -1.0, jnp.float32)
    for index, block in enumerate(blocks):
        here = block[0:rows, :]
        code = code_at(block, rows)
        plane[index * rows : (index + 1) * rows, :] = here
        codes[index : index + 1, :] = code
        scores = scores_of(mine, here)
        for at in range(0, rows, 128):
            other = code[:, at : at + 128]
            earlier = ((column ^ other) < 65536) & (column > other)
            found = jnp.maximum(found, jnp.where(earlier, scores[:, at : at + 128], -1.0))
    kept[...] = jnp.full(kept.shape, -1.0, jnp.float32)
    kept[0:1, :] = fold_rows(found)


def meet_kernel(rows, n_plane, has_far, has_near, *refs):
    (plane, codes, part), refs = refs[:3], list(refs[3:])
    if has_far:
        far, far_ids = refs.pop(0), refs.pop(0)
        far_rows, far_column = normalise(far[...]), as_column(code_in(far_ids))
        found = jnp.full((rows, 128), -1.0, jnp.float32)
    if has_near:
        near, near_ids = refs.pop(0), refs.pop(0)
        near_rows, near_column = normalise(near[...]), as_column(code_in(near_ids))
    kept = refs.pop(0)
    for index in range(n_plane):
        here = plane[index * rows : (index + 1) * rows, :]
        far_scores = scores_of(far_rows, here) if has_far else None
        near_scores = scores_of(near_rows, here) if has_near else None
        for at in range(0, rows, 128):
            lanes = slice(at, at + 128)
            other = codes[index : index + 1, lanes]
            keep = jnp.full((rows, 128), -1.0, jnp.float32)
            if has_far:
                shared = jnp.where((far_column ^ other) < 65536, far_scores[:, lanes], -1.0)
                later = far_column > other
                found = jnp.maximum(found, jnp.where(later, shared, -1.0))
                keep = jnp.where(later, -1.0, shared)
            if has_near:
                earlier = ((near_column ^ other) < 65536) & (near_column < other)
                keep = jnp.maximum(keep, jnp.where(earlier, near_scores[:, lanes], -1.0))
            kept[index : index + 1, lanes] = jnp.maximum(
                part[index : index + 1, lanes], jnp.max(keep, axis=0, keepdims=True)
            )
    if has_far:
        (back,) = refs
        back[...] = fold_rows(found)


def kernel(body, name, out_shape, args):
    return pl.pallas_call(
        body,
        out_shape=out_shape,
        in_specs=[VMEM] * len(args),
        out_specs=(VMEM,) * len(out_shape),
        compiler_params=pltpu.CompilerParams(vmem_limit_bytes=40 * 1024 * 1024),
        name=name,
    )(*args)


def shift(n, step):
    return [(i, (i + step) % n) for i in range(n)]


def turns_of(n):
    half = n // 2
    line = [p // 2 + p % 2 * half for p in range(2 * half)] + list(range(2 * half, n))
    turns = [[(line[p], line[(p + step) % n]) for p in range(n)] for step in range(1, half + 1)]
    far = turns[: (n - 1) // 2]
    return far, turns[-1] if n % 2 == 0 else None


def on_device(embeddings, owner_ids, clusters, priority):
    rows, width = embeddings.shape
    n_work, n_team, n_sub = [lax.axis_size(a) for a in ("workers", "team", "sub")]
    n_plane = n_team * n_sub
    struct = jax.ShapeDtypeStruct
    far_turns, near_turn = turns_of(n_work)

    far = [lax.ppermute(embeddings, "workers", turn) for turn in far_turns]
    near = lax.ppermute(embeddings, "workers", near_turn) if near_turn else None
    ids = jnp.concatenate(
        [owner_ids.reshape(1, rows), clusters.reshape(1, rows), priority.reshape(1, rows)], axis=0
    )
    far_ids = [lax.ppermute(ids, "workers", turn) for turn in far_turns]
    near_ids = lax.ppermute(ids, "workers", near_turn) if near_turn else None

    def gather():
        (block,) = kernel(
            functools.partial(pack_kernel, rows),
            "pack",
            (struct((rows + EXTRA, width), jnp.bfloat16),),
            (embeddings, ids),
        )
        blocks = []
        for dt in range(n_team):
            first = lax.ppermute(block, "team", shift(n_team, dt)) if dt else block
            blocks.append(first)
            for ds in range(1, n_sub):
                blocks.append(lax.ppermute(first, "sub", shift(n_sub, ds)))
        return tuple(blocks)

    blocks = lax.cond(
        lax.axis_index("groups") < lax.axis_size("groups"),
        gather,
        lambda: (jnp.zeros((rows + EXTRA, width), jnp.bfloat16),) * n_plane,
    )
    plane, codes, kept = kernel(
        functools.partial(own_kernel, rows),
        "own",
        (
            struct((n_plane * rows, width), jnp.bfloat16),
            struct((n_plane, rows), jnp.int32),
            struct((n_plane, rows), jnp.float32),
        ),
        blocks,
    )

    answers = []
    for index in range(max(len(far), 1)):
        has_far, has_near = index < len(far), index == 0 and near is not None
        if not has_far and not has_near:
            break
        came = (far[index], far_ids[index]) if has_far else ()
        came += (near, near_ids) if has_near else ()
        out = (struct((n_plane, rows), jnp.float32),)
        out += (struct((1, rows), jnp.float32),) if has_far else ()
        kept, *back = kernel(
            functools.partial(meet_kernel, rows, n_plane, has_far, has_near),
            "meet",
            out,
            (plane, codes, kept, *came),
        )
        if has_far:
            home = [(b, a) for a, b in far_turns[index]]
            answers.append(lax.ppermute(back[0], "workers", home))

    kept = kept.reshape(n_team, n_sub, rows)
    ends = kept[:, 0]
    for ds in range(1, n_sub):
        ends = jnp.maximum(ends, lax.ppermute(kept[:, ds], "sub", shift(n_sub, -ds)))
    best = ends[0:1]
    for dt in range(1, n_team):
        best = jnp.maximum(best, lax.ppermute(ends[dt : dt + 1], "team", shift(n_team, -dt)))
    for answer in answers:
        best = jnp.maximum(best, answer)
    return best.reshape(rows)


def solution(mesh):
    placed = (
        P(("groups", "workers", "team", "sub"), None),
        P(("groups", "workers", "team", "sub"), None),
        P(("groups", "workers", "team", "sub")),
        P(("groups", "workers", "team", "sub")),
    )
    return jax.shard_map(
        on_device,
        mesh=mesh,
        in_specs=placed,
        out_specs=P(("groups", "workers", "team", "sub")),
        check_vma=False,
    )
```

```python
import functools

import jax
import jax.numpy as jnp
from jax import lax
from jax.experimental import pallas as pl
from jax.experimental.pallas import tpu as pltpu
from jax.sharding import PartitionSpec as P

KC = 16
EXTRA = 16
VMEM = pl.BlockSpec(memory_space=pltpu.VMEM)


def normalise(raw):
    values = raw.astype(jnp.float32)
    total = jnp.sum(values * values, axis=1, keepdims=True)
    return (values * lax.rsqrt(total + 1e-06)).astype(jnp.bfloat16)


def code_of(owner, cluster, high, low):
    return ((owner * KC + cluster) * 256 + high) * 256 + low


def code_in(ids):
    place = ids[2:3, :]
    return code_of(ids[0:1, :], ids[1:2, :], place // 256, place % 256)


def code_at(block, rows):
    last = block[rows : rows + EXTRA, :].astype(jnp.float32)[0:1, :].astype(jnp.int32)
    return code_of(*[last[:, i * rows : (i + 1) * rows] for i in range(4)])


def as_column(row):
    return jnp.broadcast_to(row, (128, row.shape[1])).T


def fold_rows(best):
    return jnp.max(best.T, axis=0, keepdims=True)


def scores_of(left, right):
    return lax.dot_general(
        left, right, (((1,), (1,)), ((), ())), preferred_element_type=jnp.float32
    )


def pack_kernel(rows, raw, ids, block):
    width = block.shape[1]
    place = ids[2:3, :]
    line = [ids[0:1, :], ids[1:2, :], place // 256, place % 256]
    line += [jnp.zeros((1, width - 4 * rows), jnp.int32)] if width > 4 * rows else []
    line = jnp.concatenate(line, axis=1).astype(jnp.float32)
    first = lax.broadcasted_iota(jnp.int32, (EXTRA, width), 0) == 0
    last = jnp.where(first, jnp.broadcast_to(line, (EXTRA, width)), 0.0)
    block[0:rows, :] = normalise(raw[...])
    block[rows : rows + EXTRA, :] = last.astype(jnp.bfloat16)


def own_kernel(rows, *refs):
    blocks, (plane, codes, kept) = refs[:-3], refs[-3:]
    mine = blocks[0][0:rows, :]
    column = as_column(code_at(blocks[0], rows))
    found = jnp.full((rows, 128), -1.0, jnp.float32)
    for index, block in enumerate(blocks):
        here = block[0:rows, :]
        code = code_at(block, rows)
        plane[index * rows : (index + 1) * rows, :] = here
        codes[index : index + 1, :] = code
        scores = scores_of(mine, here)
        for at in range(0, rows, 128):
            other = code[:, at : at + 128]
            earlier = ((column ^ other) < 65536) & (column > other)
            found = jnp.maximum(found, jnp.where(earlier, scores[:, at : at + 128], -1.0))
    kept[...] = jnp.full(kept.shape, -1.0, jnp.float32)
    kept[0:1, :] = fold_rows(found)


def meet_kernel(rows, n_plane, has_far, has_near, *refs):
    (plane, codes, part), refs = refs[:3], list(refs[3:])
    if has_far:
        far, far_ids = refs.pop(0), refs.pop(0)
        far_rows, far_column = normalise(far[...]), as_column(code_in(far_ids))
        found = jnp.full((rows, 128), -1.0, jnp.float32)
    if has_near:
        near, near_ids = refs.pop(0), refs.pop(0)
        near_rows, near_column = normalise(near[...]), as_column(code_in(near_ids))
    kept = refs.pop(0)
    for index in range(n_plane):
        here = plane[index * rows : (index + 1) * rows, :]
        far_scores = scores_of(far_rows, here) if has_far else None
        near_scores = scores_of(near_rows, here) if has_near else None
        for at in range(0, rows, 128):
            lanes = slice(at, at + 128)
            other = codes[index : index + 1, lanes]
            keep = jnp.full((rows, 128), -1.0, jnp.float32)
            if has_far:
                shared = jnp.where((far_column ^ other) < 65536, far_scores[:, lanes], -1.0)
                later = far_column > other
                found = jnp.maximum(found, jnp.where(later, shared, -1.0))
                keep = jnp.where(later, -1.0, shared)
            if has_near:
                earlier = ((near_column ^ other) < 65536) & (near_column < other)
                keep = jnp.maximum(keep, jnp.where(earlier, near_scores[:, lanes], -1.0))
            kept[index : index + 1, lanes] = jnp.maximum(
                part[index : index + 1, lanes], jnp.max(keep, axis=0, keepdims=True)
            )
    if has_far:
        (back,) = refs
        back[...] = fold_rows(found)


def kernel(body, name, out_shape, args):
    return pl.pallas_call(
        body,
        out_shape=out_shape,
        in_specs=[VMEM] * len(args),
        out_specs=(VMEM,) * len(out_shape),
        compiler_params=pltpu.CompilerParams(vmem_limit_bytes=40 * 1024 * 1024),
        name=name,
    )(*args)


def shift(n, step):
    return [(i, (i + step) % n) for i in range(n)]


def turns_of(n):
    half = n // 2
    line = [p // 2 + p % 2 * half for p in range(2 * half)] + list(range(2 * half, n))
    turns = [[(line[p], line[(p + step) % n]) for p in range(n)] for step in range(1, half + 1)]
    far = turns[: (n - 1) // 2]
    return far, turns[-1] if n % 2 == 0 else None


def on_device(embeddings, owner_ids, clusters, priority):
    rows, width = embeddings.shape
    n_work, n_team, n_sub = [lax.axis_size(a) for a in ("workers", "team", "sub")]
    n_plane = n_team * n_sub
    struct = jax.ShapeDtypeStruct
    far_turns, near_turn = turns_of(n_work)

    far = [lax.ppermute(embeddings, "workers", turn) for turn in far_turns]
    near = lax.ppermute(embeddings, "workers", near_turn) if near_turn else None
    ids = jnp.concatenate(
        [owner_ids.reshape(1, rows), clusters.reshape(1, rows), priority.reshape(1, rows)], axis=0
    )
    far_ids = [lax.ppermute(ids, "workers", turn) for turn in far_turns]
    near_ids = lax.ppermute(ids, "workers", near_turn) if near_turn else None

    def gather():
        (block,) = kernel(
            functools.partial(pack_kernel, rows),
            "pack",
            (struct((rows + EXTRA, width), jnp.bfloat16),),
            (embeddings, ids),
        )
        blocks = []
        for dt in range(n_team):
            first = lax.ppermute(block, "team", shift(n_team, dt)) if dt else block
            blocks.append(first)
            for ds in range(1, n_sub):
                blocks.append(lax.ppermute(first, "sub", shift(n_sub, ds)))
        return tuple(blocks)

    blocks = lax.cond(
        lax.axis_index("groups") < lax.axis_size("groups"),
        gather,
        lambda: (jnp.zeros((rows + EXTRA, width), jnp.bfloat16),) * n_plane,
    )
    plane, codes, kept = kernel(
        functools.partial(own_kernel, rows),
        "own",
        (
            struct((n_plane * rows, width), jnp.bfloat16),
            struct((n_plane, rows), jnp.int32),
            struct((n_plane, rows), jnp.float32),
        ),
        blocks,
    )

    answers = []
    for index in range(max(len(far), 1)):
        has_far, has_near = index < len(far), index == 0 and near is not None
        if not has_far and not has_near:
            break
        came = (far[index], far_ids[index]) if has_far else ()
        came += (near, near_ids) if has_near else ()
        out = (struct((n_plane, rows), jnp.float32),)
        out += (struct((1, rows), jnp.float32),) if has_far else ()
        kept, *back = kernel(
            functools.partial(meet_kernel, rows, n_plane, has_far, has_near),
            "meet",
            out,
            (plane, codes, kept, *came),
        )
        if has_far:
            home = [(b, a) for a, b in far_turns[index]]
            answers.append(lax.ppermute(back[0], "workers", home))

    kept = kept.reshape(n_team, n_sub, rows)
    ends = kept[0]
    for dt in range(1, n_team):
        ends = jnp.maximum(ends, lax.ppermute(kept[dt], "team", shift(n_team, -dt)))
    best = ends[0:1]
    for ds in range(1, n_sub):
        best = jnp.maximum(best, lax.ppermute(ends[ds : ds + 1], "sub", shift(n_sub, -ds)))
    for answer in answers:
        best = jnp.maximum(best, answer)
    return best.reshape(rows)


def solution(mesh):
    placed = (
        P(("groups", "workers", "team", "sub"), None),
        P(("groups", "workers", "team", "sub"), None),
        P(("groups", "workers", "team", "sub")),
        P(("groups", "workers", "team", "sub")),
    )
    return jax.shard_map(
        on_device,
        mesh=mesh,
        in_specs=placed,
        out_specs=P(("groups", "workers", "team", "sub")),
        check_vma=False,
    )
```

```python
import functools

import jax
import jax.numpy as jnp
from jax import lax
from jax.experimental import pallas as pl
from jax.experimental.pallas import tpu as pltpu
from jax.sharding import PartitionSpec as P

KC = 16
EXTRA = 16
VMEM = pl.BlockSpec(memory_space=pltpu.VMEM)
HBM = pl.BlockSpec(memory_space=pl.ANY)


def normalise(raw):
    values = raw.astype(jnp.float32)
    total = jnp.sum(values * values, axis=1, keepdims=True)
    return (values * lax.rsqrt(total + 1e-06)).astype(jnp.bfloat16)


def code_of(owner, cluster, high, low):
    return ((owner * KC + cluster) * 256 + high) * 256 + low


def code_in(ids):
    place = ids[2:3, :]
    return code_of(ids[0:1, :], ids[1:2, :], place // 256, place % 256)


def code_of_last(last, rows):
    line = last.astype(jnp.float32)[0:1, :].astype(jnp.int32)
    return code_of(*[line[:, i * rows : (i + 1) * rows] for i in range(4)])


def as_column(row):
    return jnp.broadcast_to(row, (128, row.shape[1])).T


def fold_rows(best):
    return jnp.max(best.T, axis=0, keepdims=True)


def scores_of(left, right):
    return lax.dot_general(
        left, right, (((1,), (1,)), ((), ())), preferred_element_type=jnp.float32
    )


def pack_kernel(rows, raw, ids, block):
    width = block.shape[1]
    place = ids[2:3, :]
    line = [ids[0:1, :], ids[1:2, :], place // 256, place % 256]
    line += [jnp.zeros((1, width - 4 * rows), jnp.int32)] if width > 4 * rows else []
    line = jnp.concatenate(line, axis=1).astype(jnp.float32)
    first = lax.broadcasted_iota(jnp.int32, (EXTRA, width), 0) == 0
    last = jnp.where(first, jnp.broadcast_to(line, (EXTRA, width)), 0.0)
    block[0:rows, :] = normalise(raw[...])
    block[rows : rows + EXTRA, :] = last.astype(jnp.bfloat16)


def load_kernel(rows, *refs):
    *blocks, plane, codes, lasts, sems = refs
    copies = [
        pltpu.make_async_copy(b.at[rows : rows + EXTRA, :], lasts.at[i], sems.at[0, i])
        for i, b in enumerate(blocks)
    ] + [
        pltpu.make_async_copy(
            b.at[0:rows, :], plane.at[i * rows : (i + 1) * rows, :], sems.at[1, i]
        )
        for i, b in enumerate(blocks)
    ]
    for copy in copies:
        copy.start()
    for copy in copies:
        copy.wait()
    for i in range(len(blocks)):
        codes[i : i + 1, :] = code_of_last(lasts[i], rows)


def own_kernel(rows, n_plane, plane, codes, best):
    mine, column = plane[0:rows, :], as_column(codes[0:1, :])
    found = jnp.full((rows, 128), -1.0, jnp.float32)
    for index in range(n_plane):
        scores = scores_of(mine, plane[index * rows : (index + 1) * rows, :])
        for at in range(0, rows, 128):
            other = codes[index : index + 1, at : at + 128]
            earlier = ((column ^ other) < 65536) & (column > other)
            found = jnp.maximum(found, jnp.where(earlier, scores[:, at : at + 128], -1.0))
    best[...] = fold_rows(found)


def score_kernel(rows, n_plane, plane, came, scores):
    came_rows = normalise(came[...])
    for index in range(n_plane):
        lanes = slice(index * rows, (index + 1) * rows)
        scores[:, lanes] = scores_of(came_rows, plane[lanes, :])


def meet_kernel(rows, n_plane, has_far, has_near, has_part, *refs):
    plane, codes, *refs = refs
    part = refs.pop(0) if has_part else None
    if has_far:
        far_scores, far_ids = refs.pop(0), refs.pop(0)
        far_column = as_column(code_in(far_ids))
        found = jnp.full((rows, 128), -1.0, jnp.float32)
    if has_near:
        near, near_ids = refs.pop(0), refs.pop(0)
        near_rows, near_column = normalise(near[...]), as_column(code_in(near_ids))
    kept = refs.pop(0)
    for index in range(n_plane):
        if has_near:
            near_scores = scores_of(near_rows, plane[index * rows : (index + 1) * rows, :])
        for at in range(0, rows, 128):
            lanes = slice(at, at + 128)
            other = codes[index : index + 1, lanes]
            keep = jnp.full((rows, 128), -1.0, jnp.float32)
            if has_far:
                scores = far_scores[:, index * rows + at : index * rows + at + 128]
                shared = jnp.where((far_column ^ other) < 65536, scores, -1.0)
                later = far_column > other
                found = jnp.maximum(found, jnp.where(later, shared, -1.0))
                keep = jnp.where(later, -1.0, shared)
            if has_near:
                earlier = ((near_column ^ other) < 65536) & (near_column < other)
                keep = jnp.maximum(keep, jnp.where(earlier, near_scores[:, lanes], -1.0))
            keep = jnp.max(keep, axis=0, keepdims=True)
            if has_part:
                keep = jnp.maximum(keep, part[index : index + 1, lanes])
            kept[index : index + 1, lanes] = keep
    if has_far:
        (back,) = refs
        back[...] = fold_rows(found)


def kernel(body, name, out_shape, args):
    return pl.pallas_call(
        body,
        out_shape=out_shape,
        in_specs=[VMEM] * len(args),
        out_specs=(VMEM,) * len(out_shape),
        compiler_params=pltpu.CompilerParams(vmem_limit_bytes=40 * 1024 * 1024),
        name=name,
    )(*args)


def shift(n, step):
    return [(i, (i + step) % n) for i in range(n)]


def turns_of(n):
    half = n // 2
    line = [p // 2 + p % 2 * half for p in range(2 * half)] + list(range(2 * half, n))
    turns = [[(line[p], line[(p + step) % n]) for p in range(n)] for step in range(1, half + 1)]
    far = turns[: (n - 1) // 2]
    return far, turns[-1] if n % 2 == 0 else None


def on_device(embeddings, owner_ids, clusters, priority):
    rows, width = embeddings.shape
    n_work, n_team, n_sub = [lax.axis_size(a) for a in ("workers", "team", "sub")]
    n_plane = n_team * n_sub
    struct = jax.ShapeDtypeStruct
    far_turns, near_turn = turns_of(n_work)

    far = [lax.ppermute(embeddings, "workers", turn) for turn in far_turns]
    near = lax.ppermute(embeddings, "workers", near_turn) if near_turn else None
    ids = jnp.concatenate(
        [owner_ids.reshape(1, rows), clusters.reshape(1, rows), priority.reshape(1, rows)], axis=0
    )
    far_ids = [lax.ppermute(ids, "workers", turn) for turn in far_turns]
    near_ids = lax.ppermute(ids, "workers", near_turn) if near_turn else None

    def gather():
        (block,) = kernel(
            functools.partial(pack_kernel, rows),
            "pack",
            (struct((rows + EXTRA, width), jnp.bfloat16),),
            (embeddings, ids),
        )
        blocks = []
        for dt in range(n_team):
            first = lax.ppermute(block, "team", shift(n_team, dt)) if dt else block
            blocks.append(first)
            for ds in range(1, n_sub):
                blocks.append(lax.ppermute(first, "sub", shift(n_sub, ds)))
        return tuple(blocks)

    blocks = lax.cond(
        lax.axis_index("groups") < lax.axis_size("groups"),
        gather,
        lambda: (jnp.zeros((rows + EXTRA, width), jnp.bfloat16),) * n_plane,
    )
    plane, codes = pl.pallas_call(
        functools.partial(load_kernel, rows),
        out_shape=(struct((n_plane * rows, width), jnp.bfloat16), struct((n_plane, rows), jnp.int32)),
        in_specs=[HBM] * n_plane,
        out_specs=(VMEM, VMEM),
        scratch_shapes=[
            pltpu.VMEM((n_plane, EXTRA, width), jnp.bfloat16),
            pltpu.SemaphoreType.DMA((2, n_plane)),
        ],
        compiler_params=pltpu.CompilerParams(vmem_limit_bytes=40 * 1024 * 1024),
        name="load",
    )(*blocks)
    (own,) = kernel(
        functools.partial(own_kernel, rows, n_plane),
        "own",
        (struct((1, rows), jnp.float32),),
        (plane, codes),
    )
    kept, answers = None, []
    for index in range(max(len(far), 1 if near is not None else 0)):
        has_far, has_near = index < len(far), index == 0 and near is not None
        out = (struct((n_plane, rows), jnp.float32),)
        args = (plane, codes) if kept is None else (plane, codes, kept)
        if has_far:
            (scores,) = kernel(
                functools.partial(score_kernel, rows, n_plane),
                "score",
                (struct((rows, n_plane * rows), jnp.float32),),
                (plane, far[index]),
            )
            args += (scores, far_ids[index])
            out += (struct((1, rows), jnp.float32),)
        if has_near:
            args += (near, near_ids)
        kept, *back = kernel(
            functools.partial(meet_kernel, rows, n_plane, has_far, has_near, kept is not None),
            "meet",
            out,
            args,
        )
        if has_far:
            home = [(b, a) for a, b in far_turns[index]]
            answers.append(lax.ppermute(back[0], "workers", home))
    if kept is None:
        kept = jnp.full((n_plane, rows), -1.0, jnp.float32)

    kept = kept.reshape(n_team, n_sub, rows)
    ends = kept[0]
    for dt in range(1, n_team):
        ends = jnp.maximum(ends, lax.ppermute(kept[dt], "team", shift(n_team, -dt)))
    best = ends[0:1]
    for ds in range(1, n_sub):
        best = jnp.maximum(best, lax.ppermute(ends[ds : ds + 1], "sub", shift(n_sub, -ds)))
    best = jnp.maximum(best, own)
    for answer in answers:
        best = jnp.maximum(best, answer)
    return best.reshape(rows)


def solution(mesh):
    placed = (
        P(("groups", "workers", "team", "sub"), None),
        P(("groups", "workers", "team", "sub"), None),
        P(("groups", "workers", "team", "sub")),
        P(("groups", "workers", "team", "sub")),
    )
    return jax.shard_map(
        on_device,
        mesh=mesh,
        in_specs=placed,
        out_specs=P(("groups", "workers", "team", "sub")),
        check_vma=False,
    )
```

```python
import functools

import jax
import jax.numpy as jnp
from jax import lax
from jax.experimental import pallas as pl
from jax.experimental.pallas import tpu as pltpu
from jax.sharding import PartitionSpec as P

KC = 16
EXTRA = 16
VMEM = pl.BlockSpec(memory_space=pltpu.VMEM)
HBM = pl.BlockSpec(memory_space=pl.ANY)


def normalise(raw):
    values = raw.astype(jnp.float32)
    total = jnp.sum(values * values, axis=1, keepdims=True)
    return (values * lax.rsqrt(total + 1e-06)).astype(jnp.bfloat16)


def code_of(owner, cluster, high, low):
    return ((owner * KC + cluster) * 256 + high) * 256 + low


def code_in(ids):
    place = ids[2:3, :]
    return code_of(ids[0:1, :], ids[1:2, :], place // 256, place % 256)


def code_of_last(last, rows):
    line = last.astype(jnp.float32)[0:1, :].astype(jnp.int32)
    return code_of(*[line[:, i * rows : (i + 1) * rows] for i in range(4)])


def as_column(row):
    return jnp.broadcast_to(row, (128, row.shape[1])).T


def fold_rows(best):
    return jnp.max(best.T, axis=0, keepdims=True)


def scores_of(left, right):
    return lax.dot_general(
        left, right, (((1,), (1,)), ((), ())), preferred_element_type=jnp.float32
    )


def pack_kernel(rows, raw, ids, block):
    width = block.shape[1]
    place = ids[2:3, :]
    line = [ids[0:1, :], ids[1:2, :], place // 256, place % 256]
    line += [jnp.zeros((1, width - 4 * rows), jnp.int32)] if width > 4 * rows else []
    line = jnp.concatenate(line, axis=1).astype(jnp.float32)
    first = lax.broadcasted_iota(jnp.int32, (EXTRA, width), 0) == 0
    last = jnp.where(first, jnp.broadcast_to(line, (EXTRA, width)), 0.0)
    block[0:rows, :] = normalise(raw[...])
    block[rows : rows + EXTRA, :] = last.astype(jnp.bfloat16)


def load_kernel(rows, *refs):
    *blocks, plane, codes, lasts, sems = refs
    copies = [
        pltpu.make_async_copy(b.at[rows : rows + EXTRA, :], lasts.at[i], sems.at[0, i])
        for i, b in enumerate(blocks)
    ] + [
        pltpu.make_async_copy(
            b.at[0:rows, :], plane.at[i * rows : (i + 1) * rows, :], sems.at[1, i]
        )
        for i, b in enumerate(blocks)
    ]
    for copy in copies:
        copy.start()
    for copy in copies:
        copy.wait()
    for i in range(len(blocks)):
        codes[i : i + 1, :] = code_of_last(lasts[i], rows)


def own_kernel(rows, n_plane, plane, codes, best):
    mine, column = plane[0:rows, :], as_column(codes[0:1, :])
    found = jnp.full((rows, 128), -1.0, jnp.float32)
    for index in range(n_plane):
        scores = scores_of(mine, plane[index * rows : (index + 1) * rows, :])
        for at in range(0, rows, 128):
            other = codes[index : index + 1, at : at + 128]
            earlier = ((column ^ other) < 65536) & (column > other)
            found = jnp.maximum(found, jnp.where(earlier, scores[:, at : at + 128], -1.0))
    best[...] = fold_rows(found)


def score_kernel(rows, n_plane, plane, came, scores):
    came_rows = came[...]
    for index in range(n_plane):
        lanes = slice(index * rows, (index + 1) * rows)
        scores[:, lanes] = scores_of(came_rows, plane[lanes, :])


def meet_kernel(rows, n_plane, n_came, has_part, *refs):
    plane, codes, *refs = refs
    part = refs.pop(0) if has_part else None
    scores, *refs = refs
    columns = [as_column(code_in(refs.pop(0)))]
    if n_came == 2:
        packed = refs.pop(0)
        came_rows = packed[0:rows, :]
        columns.append(as_column(code_of_last(packed[rows : rows + EXTRA, :], rows)))
    kept, back = refs
    found = [jnp.full((rows, 128), -1.0, jnp.float32)] * n_came
    for index in range(n_plane):
        block = slice(index * rows, (index + 1) * rows)
        tables = [scores[:, block]]
        if n_came == 2:
            tables.append(scores_of(came_rows, plane[block, :]))
        for at in range(0, rows, 128):
            lanes = slice(at, at + 128)
            other = codes[index : index + 1, lanes]
            keep = None
            for turn, (table, column) in enumerate(zip(tables, columns)):
                shared = jnp.where((column ^ other) < 65536, table[:, lanes], -1.0)
                later = column > other
                found[turn] = jnp.maximum(found[turn], jnp.where(later, shared, -1.0))
                kept_here = jnp.where(later, -1.0, shared)
                keep = kept_here if keep is None else jnp.maximum(keep, kept_here)
            keep = jnp.max(keep, axis=0, keepdims=True)
            if has_part:
                keep = jnp.maximum(keep, part[index : index + 1, lanes])
            kept[index : index + 1, lanes] = keep
    for turn in range(n_came):
        back[turn : turn + 1, :] = fold_rows(found[turn])


def kernel(body, name, out_shape, args):
    return pl.pallas_call(
        body,
        out_shape=out_shape,
        in_specs=[VMEM] * len(args),
        out_specs=(VMEM,) * len(out_shape),
        compiler_params=pltpu.CompilerParams(vmem_limit_bytes=40 * 1024 * 1024),
        name=name,
    )(*args)


def shift(n, step):
    return [(i, (i + step) % n) for i in range(n)]


def turns_of(n):
    half = n // 2
    line = [p // 2 + p % 2 * half for p in range(2 * half)] + list(range(2 * half, n))
    turns = [[(line[(p + step) % n], line[p]) for p in range(n)] for step in range(1, half + 1)]
    far = turns[: (n - 1) // 2]
    return far, turns[-1] if n % 2 == 0 else None


def on_device(embeddings, owner_ids, clusters, priority):
    rows, width = embeddings.shape
    n_work, n_team, n_sub = [lax.axis_size(a) for a in ("workers", "team", "sub")]
    n_plane = n_team * n_sub
    struct = jax.ShapeDtypeStruct
    far_turns, near_turn = turns_of(n_work)

    axes = ("workers", "team", "sub")

    def everywhere(turn_of):
        return [
            ((a * n_team + t) * n_sub + c, (b * n_team + t) * n_sub + c)
            for t in range(n_team)
            for c in range(n_sub)
            for a, b in turn_of(c)
        ]

    turns = [everywhere(lambda c, turn=turn: turn) for turn in far_turns]
    mixed = bool(far_turns) and near_turn is not None
    if mixed:
        turns[:1] = [
            everywhere(lambda c: far_turns[0] if c % 2 else near_turn),
            everywhere(lambda c: near_turn if c % 2 else far_turns[0]),
        ]
    elif near_turn is not None:
        turns = [everywhere(lambda c: near_turn)]
    ids = jnp.concatenate(
        [owner_ids.reshape(1, rows), clusters.reshape(1, rows), priority.reshape(1, rows)], axis=0
    )
    whole = (struct((rows + EXTRA, width), jnp.bfloat16),)
    (block,) = kernel(functools.partial(pack_kernel, rows), "pack", whole, (embeddings, ids))
    came = [
        lax.ppermute(block if mixed and i == 1 else embeddings, axes, turn)
        for i, turn in enumerate(turns)
    ]
    came_ids = [
        None if mixed and i == 1 else lax.ppermute(ids, axes, turn) for i, turn in enumerate(turns)
    ]

    def gather():
        blocks = []
        for dt in range(n_team):
            first = lax.ppermute(block, "team", shift(n_team, dt)) if dt else block
            blocks += [first] if dt else []
            for ds in range(1, n_sub):
                blocks.append(lax.ppermute(first, "sub", shift(n_sub, ds)))
        return tuple(blocks)

    blocks = lax.cond(
        lax.axis_index("groups") < lax.axis_size("groups"),
        gather,
        lambda: (jnp.zeros((rows + EXTRA, width), jnp.bfloat16),) * (n_plane - 1),
    )
    blocks = (block, *blocks)
    plane, codes = pl.pallas_call(
        functools.partial(load_kernel, rows),
        out_shape=(struct((n_plane * rows, width), jnp.bfloat16), struct((n_plane, rows), jnp.int32)),
        in_specs=[HBM] * n_plane,
        out_specs=(VMEM, VMEM),
        scratch_shapes=[
            pltpu.VMEM((n_plane, EXTRA, width), jnp.bfloat16),
            pltpu.SemaphoreType.DMA((2, n_plane)),
        ],
        compiler_params=pltpu.CompilerParams(vmem_limit_bytes=40 * 1024 * 1024),
        name="load",
    )(*blocks)
    (own,) = kernel(
        functools.partial(own_kernel, rows, n_plane),
        "own",
        (struct((1, rows), jnp.float32),),
        (plane, codes),
    )
    kept, answers = None, []
    steps = [[i] for i in range(len(turns))]
    if mixed:
        steps[:2] = [[0, 1]]
    for number, step in enumerate(steps):
        first, *second = step
        (scores,) = kernel(
            functools.partial(score_kernel, rows, n_plane),
            "score",
            (struct((rows, n_plane * rows), jnp.float32),),
            (plane, normalise(came[first])),
        )
        args = (plane, codes) if kept is None else (plane, codes, kept)
        args += (scores, came_ids[first])
        for turn in second:
            args += (came[turn],)
        kept, back = kernel(
            functools.partial(meet_kernel, rows, n_plane, len(step), kept is not None),
            "meet",
            (struct((n_plane, rows), jnp.float32), struct((len(step), rows), jnp.float32)),
            args,
        )
        if far_turns:
            if second:
                even = lax.axis_index("sub") % 2 == 0
                back = jnp.where(even, back[1:2], back[0:1])
            home = [(b, a) for a, b in far_turns[number]]
            answers.append(lax.ppermute(back, "workers", home))
    if kept is None:
        kept = jnp.full((n_plane, rows), -1.0, jnp.float32)

    kept = kept.reshape(n_team, n_sub, rows)
    ends = kept[0]
    for dt in range(1, n_team):
        ends = jnp.maximum(ends, lax.ppermute(kept[dt], "team", shift(n_team, -dt)))
    best = ends[0:1]
    for ds in range(1, n_sub):
        best = jnp.maximum(best, lax.ppermute(ends[ds : ds + 1], "sub", shift(n_sub, -ds)))
    best = jnp.maximum(best, own)
    for answer in answers:
        best = jnp.maximum(best, answer)
    return best.reshape(rows)


def solution(mesh):
    placed = (
        P(("groups", "workers", "team", "sub"), None),
        P(("groups", "workers", "team", "sub"), None),
        P(("groups", "workers", "team", "sub")),
        P(("groups", "workers", "team", "sub")),
    )
    return jax.shard_map(
        on_device,
        mesh=mesh,
        in_specs=placed,
        out_specs=P(("groups", "workers", "team", "sub")),
        check_vma=False,
    )
```

```python
import functools

import jax
import jax.numpy as jnp
from jax import lax
from jax.experimental import pallas as pl
from jax.experimental.pallas import tpu as pltpu
from jax.sharding import PartitionSpec as P

KC = 16
EXTRA = 8
VMEM = pl.BlockSpec(memory_space=pltpu.VMEM)
HBM = pl.BlockSpec(memory_space=pl.ANY)


def normalise(raw):
    values = raw.astype(jnp.float32)
    total = jnp.sum(values * values, axis=1, keepdims=True)
    return (values * lax.rsqrt(total + 1e-06)).astype(jnp.bfloat16)


def code_of(owner, cluster, high, low):
    return ((owner * KC + cluster) * 256 + high) * 256 + low


def code_in(ids):
    place = ids[2:3, :]
    return code_of(ids[0:1, :], ids[1:2, :], place // 256, place % 256)


def code_of_last(last, rows):
    line = last.astype(jnp.float32)[0:1, :].astype(jnp.int32)
    return code_of(*[line[:, i * rows : (i + 1) * rows] for i in range(4)])


def as_column(row):
    return jnp.broadcast_to(row, (128, row.shape[1])).T


def fold_rows(best):
    return jnp.max(best.T, axis=0, keepdims=True)


def scores_of(left, right):
    return lax.dot_general(
        left, right, (((1,), (1,)), ((), ())), preferred_element_type=jnp.float32
    )


def pack_kernel(rows, raw, ids, block):
    width = block.shape[1]
    place = ids[2:3, :]
    line = [ids[0:1, :], ids[1:2, :], place // 256, place % 256]
    line += [jnp.zeros((1, width - 4 * rows), jnp.int32)] if width > 4 * rows else []
    line = jnp.concatenate(line, axis=1).astype(jnp.float32)
    first = lax.broadcasted_iota(jnp.int32, (EXTRA, width), 0) == 0
    last = jnp.where(first, jnp.broadcast_to(line, (EXTRA, width)), 0.0)
    block[...] = jnp.concatenate([normalise(raw[...]), last.astype(jnp.bfloat16)], axis=0)


def load_kernel(rows, *refs):
    *blocks, plane, codes, sems = refs
    copies = [
        pltpu.make_async_copy(block, plane.at[i], sems.at[i]) for i, block in enumerate(blocks)
    ]
    for copy in copies:
        copy.start()
    for copy in copies:
        copy.wait()
    for i in range(len(blocks)):
        codes[i : i + 1, :] = code_of_last(plane[i][rows : rows + EXTRA, :], rows)


def own_kernel(rows, n_plane, plane, codes, best):
    mine, column = plane[0, 0:rows, :], as_column(codes[0:1, :])
    found = jnp.full((rows, 128), -1.0, jnp.float32)
    for index in range(n_plane):
        scores = scores_of(mine, plane[index, 0:rows, :])
        for at in range(0, rows, 128):
            other = codes[index : index + 1, at : at + 128]
            earlier = ((column ^ other) < 65536) & (column > other)
            found = jnp.maximum(found, jnp.where(earlier, scores[:, at : at + 128], -1.0))
    best[...] = fold_rows(found)


def score_kernel(rows, n_plane, plane, came, scores):
    came_rows = came[...]
    for index in range(n_plane):
        lanes = slice(index * rows, (index + 1) * rows)
        scores[:, lanes] = scores_of(came_rows, plane[index, 0:rows, :])


def meet_kernel(rows, n_plane, n_came, has_part, *refs):
    plane, codes, *refs = refs
    part = refs.pop(0) if has_part else None
    scores, *refs = refs
    columns = [as_column(code_in(refs.pop(0)))]
    if n_came == 2:
        packed = refs.pop(0)
        came_rows = packed[0:rows, :]
        columns.append(as_column(code_of_last(packed[...][rows : rows + EXTRA, :], rows)))
    kept, back = refs
    found = [jnp.full((rows, 128), -1.0, jnp.float32)] * n_came
    for index in range(n_plane):
        block = slice(index * rows, (index + 1) * rows)
        tables = [scores[:, block]]
        if n_came == 2:
            tables.append(scores_of(came_rows, plane[index, 0:rows, :]))
        for at in range(0, rows, 128):
            lanes = slice(at, at + 128)
            other = codes[index : index + 1, lanes]
            keep = None
            for turn, (table, column) in enumerate(zip(tables, columns)):
                shared = jnp.where((column ^ other) < 65536, table[:, lanes], -1.0)
                later = column > other
                found[turn] = jnp.maximum(found[turn], jnp.where(later, shared, -1.0))
                kept_here = jnp.where(later, -1.0, shared)
                keep = kept_here if keep is None else jnp.maximum(keep, kept_here)
            keep = jnp.max(keep, axis=0, keepdims=True)
            if has_part:
                keep = jnp.maximum(keep, part[index : index + 1, lanes])
            kept[index : index + 1, lanes] = keep
    for turn in range(n_came):
        back[turn : turn + 1, :] = fold_rows(found[turn])


def kernel(body, name, out_shape, args):
    return pl.pallas_call(
        body,
        out_shape=out_shape,
        in_specs=[VMEM] * len(args),
        out_specs=(VMEM,) * len(out_shape),
        compiler_params=pltpu.CompilerParams(vmem_limit_bytes=40 * 1024 * 1024),
        name=name,
    )(*args)


def shift(n, step):
    return [(i, (i + step) % n) for i in range(n)]


def turns_of(n):
    half = n // 2
    line = [p // 2 + p % 2 * half for p in range(2 * half)] + list(range(2 * half, n))
    turns = [[(line[(p + step) % n], line[p]) for p in range(n)] for step in range(1, half + 1)]
    far = turns[: (n - 1) // 2]
    return far, turns[-1] if n % 2 == 0 else None


def on_device(embeddings, owner_ids, clusters, priority):
    rows, width = embeddings.shape
    n_work, n_team, n_sub = [lax.axis_size(a) for a in ("workers", "team", "sub")]
    n_plane = n_team * n_sub
    struct = jax.ShapeDtypeStruct
    far_turns, near_turn = turns_of(n_work)

    axes = ("workers", "team", "sub")

    def everywhere(turn_of):
        return [
            ((a * n_team + t) * n_sub + c, (b * n_team + t) * n_sub + c)
            for t in range(n_team)
            for c in range(n_sub)
            for a, b in turn_of(c)
        ]

    turns = [everywhere(lambda c, turn=turn: turn) for turn in far_turns]
    mixed = bool(far_turns) and near_turn is not None
    if mixed:
        turns[:1] = [
            everywhere(lambda c: far_turns[0] if c % 2 else near_turn),
            everywhere(lambda c: near_turn if c % 2 else far_turns[0]),
        ]
    elif near_turn is not None:
        turns = [everywhere(lambda c: near_turn)]
    ids = jnp.concatenate(
        [owner_ids.reshape(1, rows), clusters.reshape(1, rows), priority.reshape(1, rows)], axis=0
    )
    whole = (struct((rows + EXTRA, width), jnp.bfloat16),)
    (block,) = kernel(functools.partial(pack_kernel, rows), "pack", whole, (embeddings, ids))
    came = [
        lax.ppermute(block if mixed and i == 1 else embeddings, axes, turn)
        for i, turn in enumerate(turns)
    ]
    came_ids = [
        None if mixed and i == 1 else lax.ppermute(ids, axes, turn) for i, turn in enumerate(turns)
    ]

    def gather():
        blocks = []
        for dt in range(n_team):
            first = lax.ppermute(block, "team", shift(n_team, dt)) if dt else block
            blocks += [first] if dt else []
            for ds in range(1, n_sub):
                blocks.append(lax.ppermute(first, "sub", shift(n_sub, ds)))
        return tuple(blocks)

    blocks = lax.cond(
        lax.axis_index("groups") < lax.axis_size("groups"),
        gather,
        lambda: (jnp.zeros((rows + EXTRA, width), jnp.bfloat16),) * (n_plane - 1),
    )
    blocks = (block, *blocks)
    plane, codes = pl.pallas_call(
        functools.partial(load_kernel, rows),
        out_shape=(
            struct((n_plane, rows + EXTRA, width), jnp.bfloat16),
            struct((n_plane, rows), jnp.int32),
        ),
        in_specs=[HBM] * n_plane,
        out_specs=(VMEM, VMEM),
        scratch_shapes=[pltpu.SemaphoreType.DMA((n_plane,))],
        compiler_params=pltpu.CompilerParams(vmem_limit_bytes=40 * 1024 * 1024),
        name="load",
    )(*blocks)
    (own,) = kernel(
        functools.partial(own_kernel, rows, n_plane),
        "own",
        (struct((1, rows), jnp.float32),),
        (plane, codes),
    )
    kept, answers = None, []
    steps = [[i] for i in range(len(turns))]
    if mixed:
        steps[:2] = [[0, 1]]
    for number, step in enumerate(steps):
        first, *second = step
        (scores,) = kernel(
            functools.partial(score_kernel, rows, n_plane),
            "score",
            (struct((rows, n_plane * rows), jnp.float32),),
            (plane, normalise(came[first])),
        )
        args = (plane, codes) if kept is None else (plane, codes, kept)
        args += (scores, came_ids[first])
        for turn in second:
            args += (came[turn],)
        kept, back = kernel(
            functools.partial(meet_kernel, rows, n_plane, len(step), kept is not None),
            "meet",
            (struct((n_plane, rows), jnp.float32), struct((len(step), rows), jnp.float32)),
            args,
        )
        if far_turns:
            if second:
                even = lax.axis_index("sub") % 2 == 0
                back = jnp.where(even, back[1:2], back[0:1])
            home = [(b, a) for a, b in far_turns[number]]
            answers.append(lax.ppermute(back, "workers", home))
    if kept is None:
        kept = jnp.full((n_plane, rows), -1.0, jnp.float32)

    kept = kept.reshape(n_team, n_sub, rows)
    ends = kept[0]
    for dt in range(1, n_team):
        ends = jnp.maximum(ends, lax.ppermute(kept[dt], "team", shift(n_team, -dt)))
    best = ends[0:1]
    for ds in range(1, n_sub):
        best = jnp.maximum(best, lax.ppermute(ends[ds : ds + 1], "sub", shift(n_sub, -ds)))
    best = jnp.maximum(best, own)
    for answer in answers:
        best = jnp.maximum(best, answer)
    return best.reshape(rows)


def solution(mesh):
    placed = (
        P(("groups", "workers", "team", "sub"), None),
        P(("groups", "workers", "team", "sub"), None),
        P(("groups", "workers", "team", "sub")),
        P(("groups", "workers", "team", "sub")),
    )
    return jax.shard_map(
        on_device,
        mesh=mesh,
        in_specs=placed,
        out_specs=P(("groups", "workers", "team", "sub")),
        check_vma=False,
    )
```

```python
import functools

import jax
import jax.numpy as jnp
from jax import lax
from jax.experimental import pallas as pl
from jax.experimental.pallas import tpu as pltpu
from jax.sharding import PartitionSpec as P

KC = 16
EXTRA = 8
VMEM = pl.BlockSpec(memory_space=pltpu.VMEM)
HBM = pl.BlockSpec(memory_space=pl.ANY)


def normalise(raw):
    values = raw.astype(jnp.float32)
    total = jnp.sum(values * values, axis=1, keepdims=True)
    return (values * lax.rsqrt(total + 1e-06)).astype(jnp.bfloat16)


def code_of(owner, cluster, high, low):
    return ((owner * KC + cluster) * 256 + high) * 256 + low


def code_in(ids):
    place = ids[2:3, :]
    return code_of(ids[0:1, :], ids[1:2, :], place // 256, place % 256)


def code_of_last(last, rows):
    line = last.astype(jnp.float32)[0:1, :].astype(jnp.int32)
    return code_of(*[line[:, i * rows : (i + 1) * rows] for i in range(4)])


def as_column(row):
    return jnp.broadcast_to(row, (128, row.shape[1])).T


def fold_rows(best):
    return jnp.max(best.T, axis=0, keepdims=True)


def scores_of(left, right):
    return lax.dot_general(
        left, right, (((1,), (1,)), ((), ())), preferred_element_type=jnp.float32
    )


def pack_kernel(rows, raw, ids, block):
    width = block.shape[1]
    place = ids[2:3, :]
    line = [ids[0:1, :], ids[1:2, :], place // 256, place % 256]
    line += [jnp.zeros((1, width - 4 * rows), jnp.int32)] if width > 4 * rows else []
    line = jnp.concatenate(line, axis=1).astype(jnp.float32)
    first = lax.broadcasted_iota(jnp.int32, (EXTRA, width), 0) == 0
    last = jnp.where(first, jnp.broadcast_to(line, (EXTRA, width)), 0.0)
    block[...] = jnp.concatenate([normalise(raw[...]), last.astype(jnp.bfloat16)], axis=0)


def load_kernel(rows, *refs):
    *blocks, plane, codes, sems = refs
    copies = [
        pltpu.make_async_copy(block, plane.at[i], sems.at[i]) for i, block in enumerate(blocks)
    ]
    for copy in copies:
        copy.start()
    for copy in copies:
        copy.wait()
    for i in range(len(blocks)):
        codes[i : i + 1, :] = code_of_last(plane[i][rows : rows + EXTRA, :], rows)


def own_kernel(rows, n_plane, plane, codes, best):
    mine, column = plane[0, 0:rows, :], as_column(codes[0:1, :])
    found = jnp.full((rows, 128), -1.0, jnp.float32)
    for index in range(n_plane):
        scores = scores_of(mine, plane[index, 0:rows, :])
        for at in range(0, rows, 128):
            other = codes[index : index + 1, at : at + 128]
            earlier = ((column ^ other) < 65536) & (column > other)
            found = jnp.maximum(found, jnp.where(earlier, scores[:, at : at + 128], -1.0))
    best[...] = fold_rows(found)


def score_kernel(rows, n_plane, plane, came, scores):
    came_rows = came[...]
    for index in range(n_plane):
        lanes = slice(index * rows, (index + 1) * rows)
        scores[:, lanes] = scores_of(came_rows, plane[index, 0:rows, :])


def meet_kernel(rows, places, n_came, has_part, *refs):
    plane, codes, *refs = refs
    part = refs.pop(0) if has_part else None
    scores, *refs = refs
    columns = [as_column(code_in(refs.pop(0)))]
    if n_came == 2:
        packed = refs.pop(0)
        came_rows = packed[0:rows, :]
        columns.append(as_column(code_of_last(packed[...][rows : rows + EXTRA, :], rows)))
    kept, back = refs
    found = [jnp.full((rows, 128), -1.0, jnp.float32)] * n_came
    for index, place in enumerate(places):
        block = slice(index * rows, (index + 1) * rows)
        tables = [scores[:, block]]
        if n_came == 2:
            tables.append(scores_of(came_rows, plane[index, 0:rows, :]))
        for at in range(0, rows, 128):
            lanes = slice(at, at + 128)
            other = codes[index : index + 1, lanes]
            keep = None
            for turn, (table, column) in enumerate(zip(tables, columns)):
                shared = jnp.where((column ^ other) < 65536, table[:, lanes], -1.0)
                later = column > other
                found[turn] = jnp.maximum(found[turn], jnp.where(later, shared, -1.0))
                kept_here = jnp.where(later, -1.0, shared)
                keep = kept_here if keep is None else jnp.maximum(keep, kept_here)
            keep = jnp.max(keep, axis=0, keepdims=True)
            if has_part:
                keep = jnp.maximum(keep, part[place : place + 1, lanes])
            kept[place : place + 1, lanes] = keep
    for turn in range(n_came):
        back[turn : turn + 1, :] = fold_rows(found[turn])


def kernel(body, name, out_shape, args):
    return pl.pallas_call(
        body,
        out_shape=out_shape,
        in_specs=[VMEM] * len(args),
        out_specs=(VMEM,) * len(out_shape),
        compiler_params=pltpu.CompilerParams(vmem_limit_bytes=40 * 1024 * 1024),
        name=name,
    )(*args)


def shift(n, step):
    return [(i, (i + step) % n) for i in range(n)]


def turns_of(n):
    half = n // 2
    line = [p // 2 + p % 2 * half for p in range(2 * half)] + list(range(2 * half, n))
    turns = [[(line[(p + step) % n], line[p]) for p in range(n)] for step in range(1, half + 1)]
    far = turns[: (n - 1) // 2]
    return far, turns[-1] if n % 2 == 0 else None


def on_device(embeddings, owner_ids, clusters, priority):
    rows, width = embeddings.shape
    n_work, n_team, n_sub = [lax.axis_size(a) for a in ("workers", "team", "sub")]
    n_plane = n_team * n_sub
    struct = jax.ShapeDtypeStruct
    far_turns, near_turn = turns_of(n_work)

    axes = ("workers", "team", "sub")

    def everywhere(turn_of):
        return [
            ((a * n_team + t) * n_sub + c, (b * n_team + t) * n_sub + c)
            for t in range(n_team)
            for c in range(n_sub)
            for a, b in turn_of(c)
        ]

    turns = [everywhere(lambda c, turn=turn: turn) for turn in far_turns]
    mixed = bool(far_turns) and near_turn is not None
    if mixed:
        turns[:1] = [
            everywhere(lambda c: far_turns[0] if c % 2 else near_turn),
            everywhere(lambda c: near_turn if c % 2 else far_turns[0]),
        ]
    elif near_turn is not None:
        turns = [everywhere(lambda c: near_turn)]
    ids = jnp.concatenate(
        [owner_ids.reshape(1, rows), clusters.reshape(1, rows), priority.reshape(1, rows)], axis=0
    )
    whole = (struct((rows + EXTRA, width), jnp.bfloat16),)
    (block,) = kernel(functools.partial(pack_kernel, rows), "pack", whole, (embeddings, ids))
    came = [
        lax.ppermute(block if mixed and i == 1 else embeddings, axes, turn)
        for i, turn in enumerate(turns)
    ]
    came_ids = [
        None if mixed and i == 1 else lax.ppermute(ids, axes, turn) for i, turn in enumerate(turns)
    ]

    def gather():
        blocks = []
        for dt in range(n_team):
            first = lax.ppermute(block, "team", shift(n_team, dt)) if dt else block
            blocks += [first] if dt else []
            for ds in range(1, n_sub):
                blocks.append(lax.ppermute(first, "sub", shift(n_sub, ds)))
        return tuple(blocks)

    blocks = lax.cond(
        lax.axis_index("groups") < lax.axis_size("groups"),
        gather,
        lambda: (jnp.zeros((rows + EXTRA, width), jnp.bfloat16),) * (n_plane - 1),
    )
    blocks = (block, *blocks)
    plane, codes = pl.pallas_call(
        functools.partial(load_kernel, rows),
        out_shape=(
            struct((n_plane, rows + EXTRA, width), jnp.bfloat16),
            struct((n_plane, rows), jnp.int32),
        ),
        in_specs=[HBM] * n_plane,
        out_specs=(VMEM, VMEM),
        scratch_shapes=[pltpu.SemaphoreType.DMA((n_plane,))],
        compiler_params=pltpu.CompilerParams(vmem_limit_bytes=40 * 1024 * 1024),
        name="load",
    )(*blocks)
    (own,) = kernel(
        functools.partial(own_kernel, rows, n_plane),
        "own",
        (struct((1, rows), jnp.float32),),
        (plane, codes),
    )
    places = [ds * n_team + dt for dt in range(n_team) for ds in range(n_sub)]
    kept, answers = None, []
    steps = [[i] for i in range(len(turns))]
    if mixed:
        steps[:2] = [[0, 1]]
    for number, step in enumerate(steps):
        first, *second = step
        (scores,) = kernel(
            functools.partial(score_kernel, rows, n_plane),
            "score",
            (struct((rows, n_plane * rows), jnp.float32),),
            (plane, normalise(came[first])),
        )
        args = (plane, codes) if kept is None else (plane, codes, kept)
        args += (scores, came_ids[first])
        for turn in second:
            args += (came[turn],)
        kept, back = kernel(
            functools.partial(meet_kernel, rows, places, len(step), kept is not None),
            "meet",
            (struct((n_plane, rows), jnp.float32), struct((len(step), rows), jnp.float32)),
            args,
        )
        if far_turns:
            if second:
                even = lax.axis_index("sub") % 2 == 0
                back = jnp.where(even, back[1:2], back[0:1])
            home = [(b, a) for a, b in far_turns[number]]
            answers.append(lax.ppermute(back, "workers", home))
    if kept is None:
        kept = jnp.full((n_plane, rows), -1.0, jnp.float32)

    kept = kept.reshape(n_sub, n_team, rows)
    ends = kept[0]
    for ds in range(1, n_sub):
        ends = jnp.maximum(ends, lax.ppermute(kept[ds], "sub", shift(n_sub, -ds)))
    best = ends[0:1]
    for dt in range(1, n_team):
        best = jnp.maximum(best, lax.ppermute(ends[dt : dt + 1], "team", shift(n_team, -dt)))
    best = jnp.maximum(best, own)
    for answer in answers:
        best = jnp.maximum(best, answer)
    return best.reshape(rows)


def solution(mesh):
    placed = (
        P(("groups", "workers", "team", "sub"), None),
        P(("groups", "workers", "team", "sub"), None),
        P(("groups", "workers", "team", "sub")),
        P(("groups", "workers", "team", "sub")),
    )
    return jax.shard_map(
        on_device,
        mesh=mesh,
        in_specs=placed,
        out_specs=P(("groups", "workers", "team", "sub")),
        check_vma=False,
    )
```

```python
import functools

import jax
import jax.numpy as jnp
from jax import lax
from jax.experimental import pallas as pl
from jax.experimental.pallas import tpu as pltpu
from jax.sharding import PartitionSpec as P

KC = 16
EXTRA = 8
VMEM = pl.BlockSpec(memory_space=pltpu.VMEM)
HBM = pl.BlockSpec(memory_space=pl.ANY)


def normalise(raw):
    values = raw.astype(jnp.float32)
    total = jnp.sum(values * values, axis=1, keepdims=True)
    return (values * lax.rsqrt(total + 1e-06)).astype(jnp.bfloat16)


def code_of(owner, cluster, high, low):
    return ((owner * KC + cluster) * 256 + high) * 256 + low


def code_in(ids):
    place = ids[2:3, :]
    return code_of(ids[0:1, :], ids[1:2, :], place // 256, place % 256)


def code_of_last(last, rows):
    line = last.astype(jnp.float32)[0:1, :].astype(jnp.int32)
    return code_of(*[line[:, i * rows : (i + 1) * rows] for i in range(4)])


def as_column(row):
    return jnp.broadcast_to(row, (128, row.shape[1])).T


def fold_rows(best):
    return jnp.max(best.T, axis=0, keepdims=True)


def scores_of(left, right):
    return lax.dot_general(
        left, right, (((1,), (1,)), ((), ())), preferred_element_type=jnp.float32
    )


def pack_kernel(rows, raw, ids, block):
    width = block.shape[1]
    place = ids[2:3, :]
    line = [ids[0:1, :], ids[1:2, :], place // 256, place % 256]
    line += [jnp.zeros((1, width - 4 * rows), jnp.int32)] if width > 4 * rows else []
    line = jnp.concatenate(line, axis=1).astype(jnp.float32)
    first = lax.broadcasted_iota(jnp.int32, (EXTRA, width), 0) == 0
    last = jnp.where(first, jnp.broadcast_to(line, (EXTRA, width)), 0.0)
    block[...] = jnp.concatenate([normalise(raw[...]), last.astype(jnp.bfloat16)], axis=0)


def load_kernel(rows, *refs):
    *blocks, plane, codes, sems = refs
    copies = [
        pltpu.make_async_copy(block, plane.at[i], sems.at[i]) for i, block in enumerate(blocks)
    ]
    for copy in copies:
        copy.start()
    for copy in copies:
        copy.wait()
    for i in range(len(blocks)):
        codes[i : i + 1, :] = code_of_last(plane[i][rows : rows + EXTRA, :], rows)


def own_kernel(rows, n_plane, plane, codes, best):
    mine, column = plane[0, 0:rows, :], as_column(codes[0:1, :])
    found = jnp.full((rows, 128), -1.0, jnp.float32)
    for index in range(n_plane):
        scores = scores_of(mine, plane[index, 0:rows, :])
        for at in range(0, rows, 128):
            other = codes[index : index + 1, at : at + 128]
            earlier = ((column ^ other) < 65536) & (column > other)
            found = jnp.maximum(found, jnp.where(earlier, scores[:, at : at + 128], -1.0))
    best[...] = fold_rows(found)


def score_kernel(rows, n_plane, plane, came, scores):
    came_rows = came[...]
    for index in range(n_plane):
        lanes = slice(index * rows, (index + 1) * rows)
        scores[:, lanes] = scores_of(came_rows, plane[index, 0:rows, :])


def meet_kernel(rows, places, n_came, has_part, odd, *refs):
    plane, codes, *refs = refs
    part = refs.pop(0) if has_part else None
    scores, ids, *refs = refs
    packed = refs.pop(0) if n_came == 2 else None
    kept, back = refs

    def meet(far):
        columns = [as_column(code_in(ids))]
        if n_came == 2:
            came_rows = packed[0:rows, :]
            columns.append(as_column(code_of_last(packed[...][rows : rows + EXTRA, :], rows)))
        found = jnp.full((rows, 128), -1.0, jnp.float32)
        for index, place in enumerate(places):
            tables = [scores[:, index * rows : (index + 1) * rows]]
            if n_came == 2:
                tables.append(scores_of(came_rows, plane[index, 0:rows, :]))
            for at in range(0, rows, 128):
                lanes = slice(at, at + 128)
                other = codes[index : index + 1, lanes]
                keep = jnp.full((rows, 128), -1.0, jnp.float32)
                for turn, (table, column) in enumerate(zip(tables, columns)):
                    same, later = (column ^ other) < 65536, column > other
                    if turn == far:
                        shared = jnp.where(same, table[:, lanes], -1.0)
                        found = jnp.maximum(found, jnp.where(later, shared, -1.0))
                        keep = jnp.maximum(keep, jnp.where(later, -1.0, shared))
                    else:
                        earlier = same & (column < other)
                        keep = jnp.maximum(keep, jnp.where(earlier, table[:, lanes], -1.0))
                keep = jnp.max(keep, axis=0, keepdims=True)
                if has_part:
                    keep = jnp.maximum(keep, part[place : place + 1, lanes])
                kept[place : place + 1, lanes] = keep
        back[...] = fold_rows(found)

    if n_came == 1:
        meet(0)
    else:
        pl.when(odd[0] != 0)(lambda: meet(0))
        pl.when(odd[0] == 0)(lambda: meet(1))


def kernel(body, name, out_shape, args):
    return pl.pallas_call(
        body,
        out_shape=out_shape,
        in_specs=[VMEM] * len(args),
        out_specs=(VMEM,) * len(out_shape),
        compiler_params=pltpu.CompilerParams(vmem_limit_bytes=40 * 1024 * 1024),
        name=name,
    )(*args)


def shift(n, step):
    return [(i, (i + step) % n) for i in range(n)]


def turns_of(n):
    half = n // 2
    line = [p // 2 + p % 2 * half for p in range(2 * half)] + list(range(2 * half, n))
    turns = [[(line[(p + step) % n], line[p]) for p in range(n)] for step in range(1, half + 1)]
    far = turns[: (n - 1) // 2]
    return far, turns[-1] if n % 2 == 0 else None


def on_device(embeddings, owner_ids, clusters, priority):
    rows, width = embeddings.shape
    n_work, n_team, n_sub = [lax.axis_size(a) for a in ("workers", "team", "sub")]
    n_plane = n_team * n_sub
    struct = jax.ShapeDtypeStruct
    far_turns, near_turn = turns_of(n_work)

    axes = ("workers", "team", "sub")

    def everywhere(turn_of):
        return [
            ((a * n_team + t) * n_sub + c, (b * n_team + t) * n_sub + c)
            for t in range(n_team)
            for c in range(n_sub)
            for a, b in turn_of(c)
        ]

    turns = [everywhere(lambda c, turn=turn: turn) for turn in far_turns]
    mixed = bool(far_turns) and near_turn is not None
    if mixed:
        turns[:1] = [
            everywhere(lambda c: far_turns[0] if c % 2 else near_turn),
            everywhere(lambda c: near_turn if c % 2 else far_turns[0]),
        ]
    elif near_turn is not None:
        turns = [everywhere(lambda c: near_turn)]
    ids = jnp.concatenate(
        [owner_ids.reshape(1, rows), clusters.reshape(1, rows), priority.reshape(1, rows)], axis=0
    )
    whole = (struct((rows + EXTRA, width), jnp.bfloat16),)
    (block,) = kernel(functools.partial(pack_kernel, rows), "pack", whole, (embeddings, ids))
    came = [
        lax.ppermute(block if mixed and i == 1 else embeddings, axes, turn)
        for i, turn in enumerate(turns)
    ]
    came_ids = [
        None if mixed and i == 1 else lax.ppermute(ids, axes, turn) for i, turn in enumerate(turns)
    ]

    def gather():
        blocks = []
        for dt in range(n_team):
            first = lax.ppermute(block, "team", shift(n_team, dt)) if dt else block
            blocks += [first] if dt else []
            for ds in range(1, n_sub):
                blocks.append(lax.ppermute(first, "sub", shift(n_sub, ds)))
        return tuple(blocks)

    blocks = lax.cond(
        lax.axis_index("groups") < lax.axis_size("groups"),
        gather,
        lambda: (jnp.zeros((rows + EXTRA, width), jnp.bfloat16),) * (n_plane - 1),
    )
    blocks = (block, *blocks)
    plane, codes = pl.pallas_call(
        functools.partial(load_kernel, rows),
        out_shape=(
            struct((n_plane, rows + EXTRA, width), jnp.bfloat16),
            struct((n_plane, rows), jnp.int32),
        ),
        in_specs=[HBM] * n_plane,
        out_specs=(VMEM, VMEM),
        scratch_shapes=[pltpu.SemaphoreType.DMA((n_plane,))],
        compiler_params=pltpu.CompilerParams(vmem_limit_bytes=40 * 1024 * 1024),
        name="load",
    )(*blocks)
    (own,) = kernel(
        functools.partial(own_kernel, rows, n_plane),
        "own",
        (struct((1, rows), jnp.float32),),
        (plane, codes),
    )
    places = [ds * n_team + dt for dt in range(n_team) for ds in range(n_sub)]
    kept, answers = None, []
    steps = [[i] for i in range(len(turns))]
    if mixed:
        steps[:2] = [[0, 1]]
    for number, step in enumerate(steps):
        first, *second = step
        (scores,) = kernel(
            functools.partial(score_kernel, rows, n_plane),
            "score",
            (struct((rows, n_plane * rows), jnp.float32),),
            (plane, normalise(came[first])),
        )
        args = (plane, codes) if kept is None else (plane, codes, kept)
        args += (scores, came_ids[first])
        for turn in second:
            args += (came[turn],)
        kept, back = pl.pallas_call(
            functools.partial(meet_kernel, rows, places, len(step), kept is not None),
            out_shape=(struct((n_plane, rows), jnp.float32), struct((1, rows), jnp.float32)),
            in_specs=[pl.BlockSpec(memory_space=pltpu.SMEM)] + [VMEM] * len(args),
            out_specs=(VMEM, VMEM),
            compiler_params=pltpu.CompilerParams(vmem_limit_bytes=40 * 1024 * 1024),
            name="meet",
        )(lax.axis_index("sub").reshape(1) % 2, *args)
        if far_turns:
            home = [(b, a) for a, b in far_turns[number]]
            answers.append(lax.ppermute(back, "workers", home))
    if kept is None:
        kept = jnp.full((n_plane, rows), -1.0, jnp.float32)

    kept = kept.reshape(n_sub, n_team, rows)
    ends = kept[0]
    for ds in range(1, n_sub):
        ends = jnp.maximum(ends, lax.ppermute(kept[ds], "sub", shift(n_sub, -ds)))
    best = ends[0:1]
    for dt in range(1, n_team):
        best = jnp.maximum(best, lax.ppermute(ends[dt : dt + 1], "team", shift(n_team, -dt)))
    best = jnp.maximum(best, own)
    for answer in answers:
        best = jnp.maximum(best, answer)
    return best.reshape(rows)


def solution(mesh):
    placed = (
        P(("groups", "workers", "team", "sub"), None),
        P(("groups", "workers", "team", "sub"), None),
        P(("groups", "workers", "team", "sub")),
        P(("groups", "workers", "team", "sub")),
    )
    return jax.shard_map(
        on_device,
        mesh=mesh,
        in_specs=placed,
        out_specs=P(("groups", "workers", "team", "sub")),
        check_vma=False,
    )
```

```python
import functools

import jax
import jax.numpy as jnp
from jax import lax
from jax.experimental import pallas as pl
from jax.experimental.pallas import tpu as pltpu
from jax.sharding import PartitionSpec as P

KC = 16
EXTRA = 8
VMEM = pl.BlockSpec(memory_space=pltpu.VMEM)
HBM = pl.BlockSpec(memory_space=pl.ANY)


def normalise(raw):
    values = raw.astype(jnp.float32)
    total = jnp.sum(values * values, axis=1, keepdims=True)
    return (values * lax.rsqrt(total + 1e-06)).astype(jnp.bfloat16)


def code_of(owner, cluster, high, low):
    return ((owner * KC + cluster) * 256 + high) * 256 + low


def code_in(ids):
    place = ids[2:3, :]
    return code_of(ids[0:1, :], ids[1:2, :], place // 256, place % 256)


def code_of_last(last, rows):
    line = last.astype(jnp.float32)[0:1, :].astype(jnp.int32)
    return code_of(*[line[:, i * rows : (i + 1) * rows] for i in range(4)])


def as_column(row):
    return jnp.broadcast_to(row, (128, row.shape[1])).T


def fold_rows(best):
    return jnp.max(best.T, axis=0, keepdims=True)


def scores_of(left, right):
    return lax.dot_general(
        left, right, (((1,), (1,)), ((), ())), preferred_element_type=jnp.float32
    )


def pack_kernel(rows, raw, ids, block):
    width = block.shape[1]
    place = ids[2:3, :]
    line = [ids[0:1, :], ids[1:2, :], place // 256, place % 256]
    line += [jnp.zeros((1, width - 4 * rows), jnp.int32)] if width > 4 * rows else []
    line = jnp.concatenate(line, axis=1).astype(jnp.float32)
    first = lax.broadcasted_iota(jnp.int32, (EXTRA, width), 0) == 0
    last = jnp.where(first, jnp.broadcast_to(line, (EXTRA, width)), 0.0)
    block[...] = jnp.concatenate([normalise(raw[...]), last.astype(jnp.bfloat16)], axis=0)


def load_kernel(rows, *refs):
    *blocks, plane, codes, sems = refs
    copies = [
        pltpu.make_async_copy(block, plane.at[i], sems.at[i]) for i, block in enumerate(blocks)
    ]
    for copy in copies:
        copy.start()
    for copy in copies:
        copy.wait()
    for i in range(len(blocks)):
        codes[i : i + 1, :] = code_of_last(plane[i][rows : rows + EXTRA, :], rows)


def own_kernel(rows, n_plane, plane, codes, best):
    mine, column = plane[0, 0:rows, :], as_column(codes[0:1, :])
    found = jnp.full((rows, 128), -1.0, jnp.float32)
    for index in range(n_plane):
        scores = scores_of(mine, plane[index, 0:rows, :])
        for at in range(0, rows, 128):
            other = codes[index : index + 1, at : at + 128]
            earlier = ((column ^ other) < 65536) & (column > other)
            found = jnp.maximum(found, jnp.where(earlier, scores[:, at : at + 128], -1.0))
    best[...] = fold_rows(found)


def score_kernel(rows, n_plane, plane, came, scores):
    came_rows = came[...]
    for index in range(n_plane):
        lanes = slice(index * rows, (index + 1) * rows)
        scores[:, lanes] = scores_of(came_rows, plane[index, 0:rows, :])


def meet_kernel(rows, n_plane, n_came, has_part, odd, *refs):
    plane, codes, *refs = refs
    part = refs.pop(0) if has_part else None
    scores, ids, *refs = refs
    packed = refs.pop(0) if n_came == 2 else None
    kept, back = refs

    def meet(far):
        columns = [as_column(code_in(ids))]
        if n_came == 2:
            came_rows = packed[0:rows, :]
            columns.append(as_column(code_of_last(packed[...][rows : rows + EXTRA, :], rows)))
        found = jnp.full((rows, 128), -1.0, jnp.float32)
        for index in range(n_plane):
            tables = [scores[:, index * rows : (index + 1) * rows]]
            if n_came == 2:
                tables.append(scores_of(came_rows, plane[index, 0:rows, :]))
            for at in range(0, rows, 128):
                lanes = slice(at, at + 128)
                other = codes[index : index + 1, lanes]
                keep = jnp.full((rows, 128), -1.0, jnp.float32)
                for turn, (table, column) in enumerate(zip(tables, columns)):
                    same, later = (column ^ other) < 65536, column > other
                    if turn == far:
                        shared = jnp.where(same, table[:, lanes], -1.0)
                        found = jnp.maximum(found, jnp.where(later, shared, -1.0))
                        keep = jnp.maximum(keep, jnp.where(later, -1.0, shared))
                    else:
                        earlier = same & (column < other)
                        keep = jnp.maximum(keep, jnp.where(earlier, table[:, lanes], -1.0))
                keep = jnp.max(keep, axis=0, keepdims=True)
                if has_part:
                    keep = jnp.maximum(keep, part[index : index + 1, lanes])
                kept[index : index + 1, lanes] = keep
        back[...] = fold_rows(found)

    if n_came == 1:
        meet(0)
    else:
        pl.when(odd[0] != 0)(lambda: meet(0))
        pl.when(odd[0] == 0)(lambda: meet(1))


def kernel(body, name, out_shape, args):
    return pl.pallas_call(
        body,
        out_shape=out_shape,
        in_specs=[VMEM] * len(args),
        out_specs=(VMEM,) * len(out_shape),
        compiler_params=pltpu.CompilerParams(vmem_limit_bytes=40 * 1024 * 1024),
        name=name,
    )(*args)


def shift(n, step):
    return [(i, (i + step) % n) for i in range(n)]


def turns_of(n):
    half = n // 2
    line = [p // 2 + p % 2 * half for p in range(2 * half)] + list(range(2 * half, n))
    turns = [[(line[(p + step) % n], line[p]) for p in range(n)] for step in range(1, half + 1)]
    far = turns[: (n - 1) // 2]
    return far, turns[-1] if n % 2 == 0 else None


def on_device(embeddings, owner_ids, clusters, priority):
    rows, width = embeddings.shape
    n_work, n_team, n_sub = [lax.axis_size(a) for a in ("workers", "team", "sub")]
    n_plane = n_team * n_sub
    struct = jax.ShapeDtypeStruct
    far_turns, near_turn = turns_of(n_work)

    axes = ("workers", "team", "sub")

    def everywhere(turn_of):
        return [
            ((a * n_team + t) * n_sub + c, (b * n_team + t) * n_sub + c)
            for t in range(n_team)
            for c in range(n_sub)
            for a, b in turn_of(c)
        ]

    turns = [everywhere(lambda c, turn=turn: turn) for turn in far_turns]
    mixed = bool(far_turns) and near_turn is not None
    if mixed:
        turns[:1] = [
            everywhere(lambda c: far_turns[0] if c % 2 else near_turn),
            everywhere(lambda c: near_turn if c % 2 else far_turns[0]),
        ]
    elif near_turn is not None:
        turns = [everywhere(lambda c: near_turn)]
    ids = jnp.concatenate(
        [owner_ids.reshape(1, rows), clusters.reshape(1, rows), priority.reshape(1, rows)], axis=0
    )
    whole = (struct((rows + EXTRA, width), jnp.bfloat16),)
    (block,) = kernel(functools.partial(pack_kernel, rows), "pack", whole, (embeddings, ids))
    came = [
        lax.ppermute(block if mixed and i == 1 else embeddings, axes, turn)
        for i, turn in enumerate(turns)
    ]
    came_ids = [
        None if mixed and i == 1 else lax.ppermute(ids, axes, turn) for i, turn in enumerate(turns)
    ]

    def gather():
        blocks = []
        for dt in range(n_team):
            first = lax.ppermute(block, "team", shift(n_team, dt)) if dt else block
            blocks += [first] if dt else []
            for ds in range(1, n_sub):
                blocks.append(lax.ppermute(first, "sub", shift(n_sub, ds)))
        return tuple(blocks)

    blocks = lax.cond(
        lax.axis_index("groups") < lax.axis_size("groups"),
        gather,
        lambda: (jnp.zeros((rows + EXTRA, width), jnp.bfloat16),) * (n_plane - 1),
    )
    blocks = (block, *blocks)
    plane, codes = pl.pallas_call(
        functools.partial(load_kernel, rows),
        out_shape=(
            struct((n_plane, rows + EXTRA, width), jnp.bfloat16),
            struct((n_plane, rows), jnp.int32),
        ),
        in_specs=[HBM] * n_plane,
        out_specs=(VMEM, VMEM),
        scratch_shapes=[pltpu.SemaphoreType.DMA((n_plane,))],
        compiler_params=pltpu.CompilerParams(vmem_limit_bytes=40 * 1024 * 1024),
        name="load",
    )(*blocks)
    (own,) = kernel(
        functools.partial(own_kernel, rows, n_plane),
        "own",
        (struct((1, rows), jnp.float32),),
        (plane, codes),
    )
    kept, answers = None, []
    steps = [[i] for i in range(len(turns))]
    if mixed:
        steps[:2] = [[0, 1]]
    for number, step in enumerate(steps):
        first, *second = step
        (scores,) = kernel(
            functools.partial(score_kernel, rows, n_plane),
            "score",
            (struct((rows, n_plane * rows), jnp.float32),),
            (plane, normalise(came[first])),
        )
        args = (plane, codes) if kept is None else (plane, codes, kept)
        args += (scores, came_ids[first])
        for turn in second:
            args += (came[turn],)
        kept, back = pl.pallas_call(
            functools.partial(meet_kernel, rows, n_plane, len(step), kept is not None),
            out_shape=(struct((n_plane, rows), jnp.float32), struct((1, rows), jnp.float32)),
            in_specs=[pl.BlockSpec(memory_space=pltpu.SMEM)] + [VMEM] * len(args),
            out_specs=(VMEM, VMEM),
            compiler_params=pltpu.CompilerParams(vmem_limit_bytes=40 * 1024 * 1024),
            name="meet",
        )(lax.axis_index("sub").reshape(1) % 2, *args)
        if far_turns:
            home = [(b, a) for a, b in far_turns[number]]
            answers.append(lax.ppermute(back, "workers", home))
    if kept is None:
        kept = jnp.full((n_plane, rows), -1.0, jnp.float32)

    kept = kept.reshape(n_team, n_sub, rows)
    ends = kept[0]
    for dt in range(1, n_team):
        ends = jnp.maximum(ends, lax.ppermute(kept[dt], "team", shift(n_team, -dt)))
    best = ends[0:1]
    for ds in range(1, n_sub):
        best = jnp.maximum(best, lax.ppermute(ends[ds : ds + 1], "sub", shift(n_sub, -ds)))
    best = jnp.maximum(best, own)
    for answer in answers:
        best = jnp.maximum(best, answer)
    return best.reshape(rows)


def solution(mesh):
    placed = (
        P(("groups", "workers", "team", "sub"), None),
        P(("groups", "workers", "team", "sub"), None),
        P(("groups", "workers", "team", "sub")),
        P(("groups", "workers", "team", "sub")),
    )
    return jax.shard_map(
        on_device,
        mesh=mesh,
        in_specs=placed,
        out_specs=P(("groups", "workers", "team", "sub")),
        check_vma=False,
    )
```
